32 devices in a mesh: chan: 8 (over z, y), win: 4 (over x, core).
Axes of the slice: x: 2, y: 2, z: 4, core: 2. Of those that a mesh axis runs over, the one named last changes fastest.
Arguments:
- spectra: bfloat16 [4, 1024, 1536], P('win', 'chan'), may hold values from -120 to 120
- masks: int32 [4, 1024], replicated, may hold values from 0 to 1, as said below
- matching: int32 [2, 8], replicated, may hold values from 0 to 7, as said below
Outputs:
- corr: bfloat16 [2, 1024, 8192], P(None, ('chan', 'win'))
The draws below stay inside these ranges and needn't reach their ends.
Inputs may be any that keep to these rules, and one draw needn't show every extreme that they name: `masks`: some channels are 0 in every window. `matching`: in round r every block i meets block i XOR s_r, with one s_r for each round, and each bit of 7 is set in exactly one of the two rounds' s_r.
All inputs are finite; a program needn't handle non-finite values.
Results may differ from the reference program's by a relative error of at most 0.014.
Values may be sent and summed in bfloat16 or wider, within the bound.
No kernel may reach another device: no remote copies, remote signals or barrier semaphores. Data moves between devices by JAX's collectives and lax.ppermute only.
A program may use at most 64 MiB of HBM per device.

```python
import math
import jax
import jax.numpy as jnp
from jax import lax

CB = 128
F = 768
LAGS = 64
ROUNDS = 2
W_DEV = 1
NBLK = 8
CHANNELS = 1024
WINDOWS = 4
N_WIN = 4


def draw_spectra(key, part):
    first_key, second_key, third_key = jax.random.split(key, 3)
    shape = (WINDOWS, CHANNELS, 2 * F)
    base = jnp.clip(jax.random.normal(first_key, shape, jnp.float32), -5.0, 5.0)
    scale = jnp.exp(jax.random.uniform(second_key, (WINDOWS, CHANNELS, 1), jnp.float32, 0.0, math.log(10.0)))
    rough = jax.random.uniform(third_key, shape, jnp.float32, 0.5, 1.5)
    return (base * scale * rough).astype(jnp.bfloat16)


def draw_masks(key, part):
    first_key, second_key = jax.random.split(jax.random.fold_in(key, 11))
    alive = jax.random.randint(first_key, (1, CHANNELS), 0, 8) != 0
    valid = jax.random.randint(second_key, (WINDOWS, CHANNELS), 0, 8) != 0
    return jnp.logical_and(alive, valid).astype(jnp.int32)


def draw_matching(key, part):
    first = jax.random.randint(jax.random.fold_in(key, 23), (), 1, NBLK - 1).astype(jnp.int32)
    flips = jnp.stack([first, jnp.bitwise_xor(first, NBLK - 1)])
    block_ids = jnp.arange(NBLK, dtype=jnp.int32)
    return jnp.bitwise_xor(block_ids[None, :], flips[:, None]).astype(jnp.int32)


def setup_inputs(seed: int = 0) -> dict:
    splits = jax.random.split(jax.random.key(seed), 4)
    return {
        "spectra": draw_spectra(jax.random.fold_in(splits[3], 71), 0),
        "masks": draw_masks(jax.random.fold_in(splits[3], 71), 0),
        "matching": draw_matching(jax.random.fold_in(splits[3], 71), 0),
    }


def tables(bin_count, lag_count):
    freq = jnp.arange(bin_count, dtype=jnp.int32)
    lag_ids = jnp.arange(lag_count, dtype=jnp.int32)
    phase = lag_ids[:, None] * freq[None, :] % (2 * bin_count)
    angle = phase.astype(jnp.float32) * (math.pi / bin_count)
    return (jnp.cos(angle), jnp.sin(angle))

def rotate(own_rows, cosine, sine):
    bin_count = cosine.shape[1]
    real_part = own_rows[..., :bin_count].astype(jnp.float32)[:, :, None, :]
    imag_part = own_rows[..., bin_count:].astype(jnp.float32)[:, :, None, :]
    turned = jnp.concatenate([real_part * cosine - imag_part * sine, real_part * sine + imag_part * cosine], axis=-1)
    turned = turned.astype(jnp.bfloat16)
    return turned.reshape(own_rows.shape[0], own_rows.shape[1] * cosine.shape[0], 2 * bin_count)

def whiten(spectra, flags):
    values = spectra.astype(jnp.float32)
    mean_square = lax.optimization_barrier(jnp.mean(values * values, axis=-1, keepdims=True))
    return (flags.astype(jnp.float32)[..., None] * values * lax.rsqrt(mean_square + 1e-06)).astype(jnp.bfloat16)

def reference(spectra, masks, matching):
    whitened = whiten(spectra, masks)
    cosine, sine = tables(F, LAGS)
    flags = masks.astype(jnp.bfloat16)

    def one_block(index):
        round_id = index // NBLK
        block_id = index % NBLK
        partner = matching[round_id, block_id]
        own_spec = lax.dynamic_slice_in_dim(whitened, (block_id * CB).astype(jnp.int32), CB, 1)
        other_spec = lax.dynamic_slice_in_dim(whitened, (partner * CB).astype(jnp.int32), CB, 1)
        own_cols = lax.dynamic_slice_in_dim(flags, (block_id * CB).astype(jnp.int32), CB, 1)
        other_cols = lax.dynamic_slice_in_dim(flags, (partner * CB).astype(jnp.int32), CB, 1)
        counts = lax.dot_general(own_cols, other_cols, (((0,), (0,)), ((), ())), preferred_element_type=jnp.float32)

        def group(running, group_id):
            first = (group_id * W_DEV).astype(jnp.int32)
            own_group = lax.dynamic_slice_in_dim(own_spec, first, W_DEV, 0)
            other_group = lax.dynamic_slice_in_dim(other_spec, first, W_DEV, 0)
            rotated = rotate(own_group, cosine, sine)
            term = jnp.einsum('wxk,wbk->xb', rotated.astype(jnp.float32), other_group.astype(jnp.float32))
            return (running + lax.optimization_barrier(term.astype(jnp.bfloat16)).astype(jnp.float32), None)
        running, _ = lax.scan(group, jnp.zeros((CB * LAGS, CB), jnp.float32), jnp.arange(N_WIN, dtype=jnp.int32))
        stacked = running.reshape(CB, LAGS, CB)
        scale = jnp.sqrt(F * jnp.maximum(counts, 1.0))
        return (stacked / scale[:, None, :]).reshape(CB, LAGS * CB).astype(jnp.bfloat16)
    result = lax.map(one_block, jnp.arange(ROUNDS * NBLK, dtype=jnp.int32))
    return result.reshape(ROUNDS, CHANNELS, LAGS * CB)
```

```python
import functools
import math

import jax
import jax.numpy as jnp
import numpy as np
from jax import lax
from jax.experimental import pallas as pl
from jax.experimental.pallas import tpu as pltpu
from jax.sharding import PartitionSpec as P

LAGS = 64
ROUNDS = 2
LAG_STEP = 16
BIN_STEP = 256
PARTS = 2
SWITCH_BLOCKS = 8

VMEM = pl.BlockSpec(memory_space=pltpu.VMEM)
SMEM = pl.BlockSpec(memory_space=pltpu.SMEM)
PARAMS = pltpu.CompilerParams(vmem_limit_bytes=56 * 2**20)


def flip(value, axis, bits):
    if bits == 0:
        return value
    return lax.ppermute(value, axis, [(i, i ^ bits) for i in range(lax.axis_size(axis))])


def tables(bin_count):
    phase = np.arange(LAGS)[:, None] * np.arange(bin_count)[None, :] % (2 * bin_count)
    angle = phase.astype(np.float64) * (math.pi / bin_count)
    return np.cos(angle).astype(np.float32), np.sin(angle).astype(np.float32)


def descending_bits(size):
    return [1 << k for k in reversed(range(size.bit_length() - 1))]


def own_rows(values):
    held = {0: values}
    count = values.shape[0]
    for bit in descending_bits(lax.axis_size("win")):
        upper = (lax.axis_index("win") & bit) != 0
        half = held[0].shape[1] // 2
        kept, sent = {}, {}
        for d, rows in held.items():
            low, high = rows[:, :half], rows[:, half:]
            kept[d] = jnp.where(upper, high, low)
            sent[d] = jnp.where(upper, low, high)
        keys = list(held)
        moved = flip(jnp.concatenate([sent[d] for d in keys], axis=0), "win", bit)
        for n, d in enumerate(keys):
            kept[d | bit] = moved[n * count : (n + 1) * count]
        held = kept
    return held


def gather_windows(values):
    held = {0: values}
    for bit in descending_bits(lax.axis_size("win")):
        for d in list(held):
            held[d | bit] = flip(held[d], "win", bit)
    return held


def prepare_kernel(spectra_ref, masks_ref, matching_ref, whole_ref, *refs):
    part_refs, pair_ref = refs[:-1], refs[-1]
    w_count, block, two_bins = spectra_ref.shape
    bins = two_bins // 2
    first = matching_ref[0, 0]
    pair_ref[0] = jnp.minimum(first, first ^ (lax.axis_size("chan") - 1))
    at = pl.ds(pl.multiple_of(lax.axis_index("chan") * block, block), block)
    every = masks_ref[:, at].astype(jnp.float32)
    for q in range(w_count):
        window = lax.axis_index("win") * w_count + q
        chosen = lax.broadcasted_iota(jnp.int32, every.shape, 0) == window
        flags = lax.dot_general(
            every,
            chosen.astype(jnp.float32),
            (((0,), (0,)), ((), ())),
            preferred_element_type=jnp.float32,
        )
        chunk = 32
        for c in range(0, block, chunk):
            values = spectra_ref[q, c : c + chunk, :].astype(jnp.float32)
            mean_square = jnp.mean(values * values, axis=-1, keepdims=True)
            factor = flags[c : c + chunk, :1] * lax.rsqrt(mean_square + 1e-06)
            white = (values * factor).astype(jnp.bfloat16)
            whole_ref[q, c : c + chunk, :] = white
            for n, part_ref in enumerate(part_refs):
                width = part_ref.shape[2] // 2
                for side in range(2):
                    part_ref[q, c : c + chunk, side * width : (side + 1) * width] = white[
                        :, side * bins + n * width : side * bins + (n + 1) * width
                    ]


def prepare(spectra, masks, matching):
    w_count, block, two_bins = spectra.shape
    shape = jax.ShapeDtypeStruct
    part = shape((w_count, block, two_bins // PARTS), jnp.bfloat16)
    outs = pl.pallas_call(
        prepare_kernel,
        out_shape=[shape(spectra.shape, jnp.bfloat16)] + [part] * PARTS + [shape((1,), jnp.int32)],
        in_specs=[VMEM, VMEM, SMEM],
        out_specs=[VMEM] * (1 + PARTS) + [SMEM],
        compiler_params=PARAMS,
    )(spectra, masks, matching)
    return outs[0], outs[1:-1], outs[-1][0]


def correlate_kernel(plan, first, last, *refs):
    refs = list(refs)
    take = lambda count: [refs.pop(0) for _ in range(count)]
    cos_ref, sin_ref = take(2)
    if first:
        masks_ref, matching_ref = take(2)
    else:
        (total_ref,) = take(1)
    if last:
        scale_ref, order_ref = take(2)
    own_refs = take(1 + max(piece[0] for piece in plan))
    left_refs = take(len(plan))
    right_refs = take(len(plan))
    rows, block = own_refs[0].shape[1], left_refs[0].shape[1]
    bins = own_refs[0].shape[2] // 2

    def dot(lhs, rhs):
        return lax.dot_general(
            lhs, rhs, (((1,), (1,)), ((), ())), preferred_element_type=jnp.float32
        )

    if first:
        new_scale_ref, counts_ref = refs[1], refs[2]
        block_id, slot = lax.axis_index("chan"), lax.axis_index("win")
        own_at = pl.ds(pl.multiple_of(block_id * block, block), block)
        own_flags = masks_ref[:, own_at].astype(jnp.float32)
        for r in range(ROUNDS):
            partner = block_id ^ matching_ref[r, 0]
            at = pl.ds(pl.multiple_of(partner * block, block), block)
            counts = lax.dot_general(
                own_flags,
                masks_ref[:, at].astype(jnp.float32),
                (((0,), (0,)), ((), ())),
                preferred_element_type=jnp.float32,
            )
            counts_ref[...] = lax.rsqrt(bins * jnp.maximum(counts, 1.0))
            new_scale_ref[r] = counts_ref[pl.ds(pl.multiple_of(slot * rows, rows), rows), :]
    out_ref = refs[0]
    if last:
        swapped = order_ref[0]
        rounds = [swapped, 1 - swapped]
        scales = [scale_ref[r] for r in rounds]

    for step in range(0, LAGS, LAG_STEP):
        total = None
        for n, (own_at, first_bin, width) in enumerate(plan):
            for q in range(own_refs[0].shape[0]):
                for c in range(0, width, BIN_STEP):
                    size = min(BIN_STEP, width - c)
                    b = first_bin + c
                    real = own_refs[own_at][q, :, b : b + size]
                    imag = own_refs[own_at][q, :, bins + b : bins + b + size]
                    cosine = cos_ref[step : step + LAG_STEP, b : b + size].astype(jnp.bfloat16)
                    sine = sin_ref[step : step + LAG_STEP, b : b + size].astype(jnp.bfloat16)
                    turned = [[], []]
                    for t in range(LAG_STEP):
                        cos, sin = cosine[t : t + 1], sine[t : t + 1]
                        turned[0].append(real * cos - imag * sin)
                        turned[1].append(real * sin + imag * cos)
                    for side in range(2):
                        at = side * width + c
                        rhs = jnp.concatenate(
                            [ref[q, :, at : at + size] for ref in (left_refs[n], right_refs[n])],
                            axis=0,
                        )
                        term = dot(jnp.concatenate(turned[side], axis=0), rhs)
                        total = term if total is None else total + term
        at = pl.ds(step * rows, LAG_STEP * rows)
        if not first:
            total = total + total_ref[at, :]
        if not last:
            out_ref[at, :] = total
            continue
        for t in range(LAG_STEP):
            lanes = pl.ds((step + t) * block, block)
            for side in range(ROUNDS):
                part = total[t * rows : (t + 1) * rows, side * block : (side + 1) * block]
                out_ref[rounds[side], :, lanes] = (part * scales[side]).astype(jnp.bfloat16)


def correlate(state, masks, matching, order, pieces, last):
    first = state is None
    own, plan = [], []
    for rows, first_bin, pair in pieces:
        if not any(rows is seen for seen in own):
            own.append(rows)
        at = next(n for n, seen in enumerate(own) if seen is rows)
        plan.append((at, first_bin, pair[0].shape[2] // 2))
    _, rows, two_bins = own[0].shape
    block = pieces[0][2][0].shape[1]
    cos, sin = tables(two_bins // 2)
    arrays = [jnp.asarray(cos), jnp.asarray(sin)]
    specs = [VMEM] * 2
    if first:
        arrays += [masks, matching]
        specs += [VMEM, SMEM]
    else:
        arrays.append(state[0])
        specs.append(VMEM)
    if last:
        arrays += [state[1], order]
        specs += [VMEM, SMEM]
    others = own + [pair[0] for *_, pair in pieces] + [pair[1] for *_, pair in pieces]
    shape = jax.ShapeDtypeStruct
    running = shape((LAGS * rows, ROUNDS * block), jnp.float32)
    if last:
        outs = [shape((ROUNDS, rows, LAGS * block), jnp.bfloat16)]
    elif first:
        outs = [running, shape((ROUNDS, rows, block), jnp.float32)]
    else:
        outs = [running]
    depth = 2 * sum(own[0].shape[0] * width for _, _, width in plan)
    result = pl.pallas_call(
        functools.partial(correlate_kernel, plan, first, last),
        out_shape=outs,
        in_specs=specs + [VMEM] * len(others),
        out_specs=[VMEM] * len(outs),
        scratch_shapes=[pltpu.VMEM((block, block), jnp.float32)] if first else [],
        compiler_params=PARAMS,
        cost_estimate=pl.CostEstimate(
            flops=2 * LAGS * rows * depth * ROUNDS * block,
            bytes_accessed=depth * (ROUNDS * block + rows) * 2,
            transcendentals=0,
        ),
    )(*arrays, *others)
    if last:
        return result[0]
    return (result[0], result[1] if first else state[1])


def combine(masks, matching, order, whole, pairs):
    own = own_rows(whole)
    gathered = [[gather_windows(side) for side in pair] for pair in pairs]
    width = pairs[0][0].shape[2] // 2
    calls = []
    groups = sorted(sorted(own)[n : n + 2] for n in range(0, len(own), 2))
    for number, group in enumerate(groups):
        parts = [
            [(own[d], n * width, [side[d] for side in gathered[n]]) for d in group]
            for n in range(len(pairs))
        ]
        calls += parts if number == len(groups) - 1 else [sum(parts, [])]
    state = None
    for number, pieces in enumerate(calls):
        state = correlate(state, masks, matching, order, pieces, number == len(calls) - 1)
    return state


def shards(spectra, masks, matching):
    blocks = lax.axis_size("chan")
    whole, parts, pair = prepare(spectra, masks, matching)

    if blocks > SWITCH_BLOCKS:
        pairs = [[part, part] for part in parts]
        for bit in range(blocks.bit_length() - 1):
            taken = (matching[0, 0] >> bit) & 1 == 1
            for n, (left, right) in enumerate(pairs):
                moved = flip(jnp.where(taken, left, right), "chan", 1 << bit)
                pairs[n] = [jnp.where(taken, moved, left), jnp.where(taken, right, moved)]
        order = jnp.zeros((1,), jnp.int32)
        return combine(masks, matching, order, whole, pairs)

    def branch(shift):
        def run(whole, parts):
            shifts = (shift, shift ^ (blocks - 1))
            pairs = [[flip(part, "chan", s) for s in shifts] for part in parts]
            order = (matching[:1, 0] != shift).astype(jnp.int32)
            return combine(masks, matching, order, whole, pairs)

        return run

    return lax.switch(pair, [branch(s) for s in range(blocks // 2)], whole, parts)


def solution(mesh):
    in_specs = (P("win", "chan", None), P(), P())
    out_specs = P(None, ("chan", "win"), None)
    return jax.shard_map(shards, mesh=mesh, in_specs=in_specs, out_specs=out_specs, check_vma=False)
```

```python
import functools
import math

import jax
import jax.numpy as jnp
import numpy as np
from jax import lax
from jax.experimental import pallas as pl
from jax.experimental.pallas import tpu as pltpu
from jax.sharding import PartitionSpec as P

LAGS = 64
ROUNDS = 2
LAG_STEP = 16
BIN_STEP = 256
PARTS = 2
SWITCH_BLOCKS = 8

VMEM = pl.BlockSpec(memory_space=pltpu.VMEM)
SMEM = pl.BlockSpec(memory_space=pltpu.SMEM)
PARAMS = pltpu.CompilerParams(vmem_limit_bytes=24 * 2**20)


def flip(value, axis, bits):
    if bits == 0:
        return value
    return lax.ppermute(value, axis, [(i, i ^ bits) for i in range(lax.axis_size(axis))])


def tables(bin_count):
    phase = np.arange(LAGS)[:, None] * np.arange(bin_count)[None, :] % (2 * bin_count)
    angle = phase.astype(np.float64) * (math.pi / bin_count)
    return np.cos(angle).astype(np.float32), np.sin(angle).astype(np.float32)


def descending_bits(size):
    return [1 << k for k in reversed(range(size.bit_length() - 1))]


def own_rows(values):
    held = {0: values}
    count = values.shape[0]
    for bit in descending_bits(lax.axis_size("win")):
        upper = (lax.axis_index("win") & bit) != 0
        half = held[0].shape[1] // 2
        kept, sent = {}, {}
        for d, rows in held.items():
            low, high = rows[:, :half], rows[:, half:]
            kept[d] = jnp.where(upper, high, low)
            sent[d] = jnp.where(upper, low, high)
        keys = list(held)
        moved = flip(jnp.concatenate([sent[d] for d in keys], axis=0), "win", bit)
        for n, d in enumerate(keys):
            kept[d | bit] = moved[n * count : (n + 1) * count]
        held = kept
    return held


def gather_windows(values):
    held = {0: values}
    for bit in descending_bits(lax.axis_size("win")):
        for d in list(held):
            held[d | bit] = flip(held[d], "win", bit)
    return held


def prepare_kernel(spectra_ref, masks_ref, matching_ref, whole_ref, *refs):
    part_refs, pair_ref = refs[:-1], refs[-1]
    w_count, block, two_bins = spectra_ref.shape
    bins = two_bins // 2
    first = matching_ref[0, 0]
    pair_ref[0] = jnp.minimum(first, first ^ (lax.axis_size("chan") - 1))
    at = pl.ds(pl.multiple_of(lax.axis_index("chan") * block, block), block)
    every = masks_ref[:, at].astype(jnp.float32)
    for q in range(w_count):
        window = lax.axis_index("win") * w_count + q
        chosen = lax.broadcasted_iota(jnp.int32, every.shape, 0) == window
        flags = lax.dot_general(
            every,
            chosen.astype(jnp.float32),
            (((0,), (0,)), ((), ())),
            preferred_element_type=jnp.float32,
        )
        chunk = 32
        for c in range(0, block, chunk):
            values = spectra_ref[q, c : c + chunk, :].astype(jnp.float32)
            mean_square = jnp.mean(values * values, axis=-1, keepdims=True)
            factor = flags[c : c + chunk, :1] * lax.rsqrt(mean_square + 1e-06)
            white = (values * factor).astype(jnp.bfloat16)
            whole_ref[q, c : c + chunk, :] = white
            for n, part_ref in enumerate(part_refs):
                width = part_ref.shape[2] // 2
                for side in range(2):
                    part_ref[q, c : c + chunk, side * width : (side + 1) * width] = white[
                        :, side * bins + n * width : side * bins + (n + 1) * width
                    ]


def prepare(spectra, masks, matching):
    w_count, block, two_bins = spectra.shape
    shape = jax.ShapeDtypeStruct
    part = shape((w_count, block, two_bins // PARTS), jnp.bfloat16)
    outs = pl.pallas_call(
        prepare_kernel,
        out_shape=[shape(spectra.shape, jnp.bfloat16)] + [part] * PARTS + [shape((1,), jnp.int32)],
        in_specs=[VMEM, VMEM, SMEM],
        out_specs=[VMEM] * (1 + PARTS) + [SMEM],
        compiler_params=PARAMS,
    )(spectra, masks, matching)
    return outs[0], outs[1:-1], outs[-1][0]


def correlate_kernel(plan, first, last, *refs):
    refs = list(refs)
    take = lambda count: [refs.pop(0) for _ in range(count)]
    cos_ref, sin_ref = take(2)
    if first:
        masks_ref, matching_ref = take(2)
    else:
        (total_ref,) = take(1)
    if last:
        scale_ref, order_ref = take(2)
    own_refs = take(1 + max(piece[0] for piece in plan))
    left_refs = take(len(plan))
    right_refs = take(len(plan))
    rows, block = own_refs[0].shape[1], left_refs[0].shape[1]
    bins = own_refs[0].shape[2] // 2

    def dot(lhs, rhs):
        return lax.dot_general(
            lhs, rhs, (((1,), (1,)), ((), ())), preferred_element_type=jnp.float32
        )

    if first:
        new_scale_ref, counts_ref = refs[1], refs[2]
        block_id, slot = lax.axis_index("chan"), lax.axis_index("win")
        own_at = pl.ds(pl.multiple_of(block_id * block, block), block)
        own_flags = masks_ref[:, own_at].astype(jnp.float32)
        for r in range(ROUNDS):
            partner = block_id ^ matching_ref[r, 0]
            at = pl.ds(pl.multiple_of(partner * block, block), block)
            counts = lax.dot_general(
                own_flags,
                masks_ref[:, at].astype(jnp.float32),
                (((0,), (0,)), ((), ())),
                preferred_element_type=jnp.float32,
            )
            counts_ref[...] = lax.rsqrt(bins * jnp.maximum(counts, 1.0))
            new_scale_ref[r] = counts_ref[pl.ds(pl.multiple_of(slot * rows, rows), rows), :]
    out_ref = refs[0]
    if last:
        swapped = order_ref[0]
        rounds = [swapped, 1 - swapped]
        scales = [scale_ref[r] for r in rounds]

    def one_step(index, carry):
        step = pl.multiple_of(index * LAG_STEP, LAG_STEP)
        total = None
        for n, (own_at, first_bin, width) in enumerate(plan):
            for q in range(own_refs[0].shape[0]):
                for c in range(0, width, BIN_STEP):
                    size = min(BIN_STEP, width - c)
                    b = first_bin + c
                    real = own_refs[own_at][q, :, b : b + size]
                    imag = own_refs[own_at][q, :, bins + b : bins + b + size]
                    cosine = cos_ref[pl.ds(step, LAG_STEP), b : b + size].astype(jnp.bfloat16)
                    sine = sin_ref[pl.ds(step, LAG_STEP), b : b + size].astype(jnp.bfloat16)
                    turned = [[], []]
                    for t in range(LAG_STEP):
                        cos, sin = cosine[t : t + 1], sine[t : t + 1]
                        turned[0].append(real * cos - imag * sin)
                        turned[1].append(real * sin + imag * cos)
                    for side in range(2):
                        at = side * width + c
                        rhs = jnp.concatenate(
                            [ref[q, :, at : at + size] for ref in (left_refs[n], right_refs[n])],
                            axis=0,
                        )
                        term = dot(jnp.concatenate(turned[side], axis=0), rhs)
                        total = term if total is None else total + term
        at = pl.ds(pl.multiple_of(step * rows, LAG_STEP * rows), LAG_STEP * rows)
        if not first:
            total = total + total_ref[at, :]
        if not last:
            out_ref[at, :] = total
            return carry
        for t in range(LAG_STEP):
            lanes = pl.ds(pl.multiple_of((step + t) * block, block), block)
            for side in range(ROUNDS):
                part = total[t * rows : (t + 1) * rows, side * block : (side + 1) * block]
                out_ref[rounds[side], :, lanes] = (part * scales[side]).astype(jnp.bfloat16)
        return carry

    lax.fori_loop(0, LAGS // LAG_STEP, one_step, 0)


def correlate(state, masks, matching, order, pieces, last):
    first = state is None
    own, plan = [], []
    for rows, first_bin, pair in pieces:
        if not any(rows is seen for seen in own):
            own.append(rows)
        at = next(n for n, seen in enumerate(own) if seen is rows)
        plan.append((at, first_bin, pair[0].shape[2] // 2))
    _, rows, two_bins = own[0].shape
    block = pieces[0][2][0].shape[1]
    cos, sin = tables(two_bins // 2)
    arrays = [jnp.asarray(cos), jnp.asarray(sin)]
    specs = [VMEM] * 2
    if first:
        arrays += [masks, matching]
        specs += [VMEM, SMEM]
    else:
        arrays.append(state[0])
        specs.append(VMEM)
    if last:
        arrays += [state[1], order]
        specs += [VMEM, SMEM]
    others = own + [pair[0] for *_, pair in pieces] + [pair[1] for *_, pair in pieces]
    shape = jax.ShapeDtypeStruct
    running = shape((LAGS * rows, ROUNDS * block), jnp.float32)
    if last:
        outs = [shape((ROUNDS, rows, LAGS * block), jnp.bfloat16)]
    elif first:
        outs = [running, shape((ROUNDS, rows, block), jnp.float32)]
    else:
        outs = [running]
    depth = 2 * sum(own[0].shape[0] * width for _, _, width in plan)
    result = pl.pallas_call(
        functools.partial(correlate_kernel, plan, first, last),
        out_shape=outs,
        in_specs=specs + [VMEM] * len(others),
        out_specs=[VMEM] * len(outs),
        scratch_shapes=[pltpu.VMEM((block, block), jnp.float32)] if first else [],
        compiler_params=PARAMS,
        cost_estimate=pl.CostEstimate(
            flops=2 * LAGS * rows * depth * ROUNDS * block,
            bytes_accessed=depth * (ROUNDS * block + rows) * 2,
            transcendentals=0,
        ),
    )(*arrays, *others)
    if last:
        return result[0]
    return (result[0], result[1] if first else state[1])


def after(values, state):
    return lax.optimization_barrier((values, state))


def combine(masks, matching, order, whole, pairs):
    own = own_rows(whole)
    width = pairs[0][0].shape[2] // 2
    low = [bit for bit in descending_bits(lax.axis_size("win"))][-1]
    high = descending_bits(lax.axis_size("win"))[:-1]
    state = None
    held = {0: pairs}
    for bit in high:
        held |= {
            d | bit: [[flip(side, "win", bit) for side in pair] for pair in held[d]] for d in list(held)
        }
    steps = [(d, n) for d in sorted(held) for n in range(len(pairs))]
    for number, (d, n) in enumerate(steps):
        pair = held[d][n]
        if state is not None:
            pair, state = after(pair, state)
        across = [flip(side, "win", low) for side in pair]
        ahead = number + 1
        if 0 < number and ahead < len(steps) and steps[ahead][0] != 0:
            d_ahead, n_ahead = steps[ahead]
            (held[d_ahead][n_ahead], across), state = after((held[d_ahead][n_ahead], across), state)
        pieces = [(own[d], n * width, pair), (own[d | low], n * width, across)]
        state = correlate(state, masks, matching, order, pieces, ahead == len(steps))
    return state


def shards(spectra, masks, matching):
    blocks = lax.axis_size("chan")
    whole, parts, pair = prepare(spectra, masks, matching)

    if blocks > SWITCH_BLOCKS:
        pairs = [[part, part] for part in parts]
        for bit in range(blocks.bit_length() - 1):
            taken = (matching[0, 0] >> bit) & 1 == 1
            for n, (left, right) in enumerate(pairs):
                moved = flip(jnp.where(taken, left, right), "chan", 1 << bit)
                pairs[n] = [jnp.where(taken, moved, left), jnp.where(taken, right, moved)]
        order = jnp.zeros((1,), jnp.int32)
        return combine(masks, matching, order, whole, pairs)

    def branch(shift):
        def run(whole, parts):
            shifts = (shift, shift ^ (blocks - 1))
            pairs = [[flip(part, "chan", s) for s in shifts] for part in parts]
            order = (matching[:1, 0] != shift).astype(jnp.int32)
            return combine(masks, matching, order, whole, pairs)

        return run

    return lax.switch(pair, [branch(s) for s in range(blocks // 2)], whole, parts)


def solution(mesh):
    in_specs = (P("win", "chan", None), P(), P())
    out_specs = P(None, ("chan", "win"), None)
    return jax.shard_map(shards, mesh=mesh, in_specs=in_specs, out_specs=out_specs, check_vma=False)
```

```python
import functools
import math

import jax
import jax.numpy as jnp
import numpy as np
from jax import lax
from jax.experimental import pallas as pl
from jax.experimental.pallas import tpu as pltpu
from jax.sharding import PartitionSpec as P

LAGS = 64
ROUNDS = 2
LAG_STEP = 16
BIN_STEP = 256
PARTS = 2
SWITCH_BLOCKS = 8

VMEM = pl.BlockSpec(memory_space=pltpu.VMEM)
SMEM = pl.BlockSpec(memory_space=pltpu.SMEM)
PARAMS = pltpu.CompilerParams(vmem_limit_bytes=24 * 2**20)


def flip(value, axis, bits):
    if bits == 0:
        return value
    return lax.ppermute(value, axis, [(i, i ^ bits) for i in range(lax.axis_size(axis))])


def tables(bin_count):
    phase = np.arange(LAGS)[:, None] * np.arange(bin_count)[None, :] % (2 * bin_count)
    angle = phase.astype(np.float64) * (math.pi / bin_count)
    return np.cos(angle).astype(np.float32), np.sin(angle).astype(np.float32)


def descending_bits(size):
    return [1 << k for k in reversed(range(size.bit_length() - 1))]


def after(values, state):
    return lax.optimization_barrier((values, state))


def own_rows(values, later):
    held = {0: values}
    count = values.shape[0]
    for bit in descending_bits(lax.axis_size("win")):
        upper = (lax.axis_index("win") & bit) != 0
        half = held[0].shape[1] // 2
        kept, sent = {}, {}
        for d, rows in held.items():
            low, high = rows[:, :half], rows[:, half:]
            kept[d] = jnp.where(upper, high, low)
            sent[d] = jnp.where(upper, low, high)
        keys = list(held)
        moved = flip(jnp.concatenate([sent[d] for d in keys], axis=0), "win", bit)
        if len(keys) == 1 and later is not None:
            moved, later = after(moved, later)
        for n, d in enumerate(keys):
            kept[d | bit] = moved[n * count : (n + 1) * count]
        held = kept
    return held, later


def prepare_kernel(spectra_ref, masks_ref, matching_ref, whole_ref, *refs):
    part_refs, pair_ref = refs[:-1], refs[-1]
    w_count, block, two_bins = spectra_ref.shape
    bins = two_bins // 2
    first = matching_ref[0, 0]
    pair_ref[0] = jnp.minimum(first, first ^ (lax.axis_size("chan") - 1))
    at = pl.ds(pl.multiple_of(lax.axis_index("chan") * block, block), block)
    every = masks_ref[:, at].astype(jnp.float32)
    for q in range(w_count):
        window = lax.axis_index("win") * w_count + q
        chosen = lax.broadcasted_iota(jnp.int32, every.shape, 0) == window
        flags = lax.dot_general(
            every,
            chosen.astype(jnp.float32),
            (((0,), (0,)), ((), ())),
            preferred_element_type=jnp.float32,
        )
        chunk = 32
        for c in range(0, block, chunk):
            values = spectra_ref[q, c : c + chunk, :].astype(jnp.float32)
            mean_square = jnp.mean(values * values, axis=-1, keepdims=True)
            factor = flags[c : c + chunk, :1] * lax.rsqrt(mean_square + 1e-06)
            white = (values * factor).astype(jnp.bfloat16)
            whole_ref[q, c : c + chunk, :] = white
            for n, part_ref in enumerate(part_refs):
                width = part_ref.shape[2] // 2
                for side in range(2):
                    part_ref[q, c : c + chunk, side * width : (side + 1) * width] = white[
                        :, side * bins + n * width : side * bins + (n + 1) * width
                    ]


def prepare(spectra, masks, matching):
    w_count, block, two_bins = spectra.shape
    shape = jax.ShapeDtypeStruct
    part = shape((w_count, block, two_bins // PARTS), jnp.bfloat16)
    outs = pl.pallas_call(
        prepare_kernel,
        out_shape=[shape(spectra.shape, jnp.bfloat16)] + [part] * PARTS + [shape((1,), jnp.int32)],
        in_specs=[VMEM, VMEM, SMEM],
        out_specs=[VMEM] * (1 + PARTS) + [SMEM],
        compiler_params=PARAMS,
    )(spectra, masks, matching)
    return outs[0], outs[1:-1], outs[-1][0]


def correlate_kernel(plan, shift, first, last, *refs):
    refs = list(refs)
    take = lambda count: [refs.pop(0) for _ in range(count)]
    cos_ref, sin_ref = take(2)
    if first:
        masks_ref, matching_ref = take(2)
    else:
        (total_ref,) = take(1)
    if last:
        scale_ref, matching_ref = take(2)
    own_refs = take(1 + max(piece[0] for piece in plan))
    stack_refs = take(len(plan))
    w_count, rows, _ = own_refs[0].shape
    block = stack_refs[0].shape[1]
    bins = own_refs[0].shape[2] // 2

    def dot(lhs, rhs):
        return lax.dot_general(
            lhs, rhs, (((1,), (1,)), ((), ())), preferred_element_type=jnp.float32
        )

    if first:
        new_scale_ref, counts_ref = refs[1], refs[2]
        block_id, slot = lax.axis_index("chan"), lax.axis_index("win")
        own_at = pl.ds(pl.multiple_of(block_id * block, block), block)
        own_flags = masks_ref[:, own_at].astype(jnp.float32)
        for r in range(ROUNDS):
            partner = block_id ^ matching_ref[r, 0]
            at = pl.ds(pl.multiple_of(partner * block, block), block)
            counts = lax.dot_general(
                own_flags,
                masks_ref[:, at].astype(jnp.float32),
                (((0,), (0,)), ((), ())),
                preferred_element_type=jnp.float32,
            )
            counts_ref[...] = lax.rsqrt(bins * jnp.maximum(counts, 1.0))
            new_scale_ref[r] = counts_ref[pl.ds(pl.multiple_of(slot * rows, rows), rows), :]
    out_ref = refs[0]
    if last:
        stage_ref, copy_sems = refs[1], refs[2]
        swapped = 0 if shift is None else jnp.where(matching_ref[0, 0] == shift, 0, 1)
        rounds = [swapped, 1 - swapped]
        scales = [scale_ref[r] for r in rounds]

    def one_step(index, carry):
        step = pl.multiple_of(index * LAG_STEP, LAG_STEP)
        total = None
        for n, (own_at, first_bin, width) in enumerate(plan):
            for q in range(w_count):
                for c in range(0, width, BIN_STEP):
                    size = min(BIN_STEP, width - c)
                    b = first_bin + c
                    real = own_refs[own_at][q, :, b : b + size]
                    imag = own_refs[own_at][q, :, bins + b : bins + b + size]
                    cosine = cos_ref[pl.ds(step, LAG_STEP), b : b + size].astype(jnp.bfloat16)
                    sine = sin_ref[pl.ds(step, LAG_STEP), b : b + size].astype(jnp.bfloat16)
                    turned = [[], []]
                    for t in range(LAG_STEP):
                        cos, sin = cosine[t : t + 1], sine[t : t + 1]
                        turned[0].append(real * cos - imag * sin)
                        turned[1].append(real * sin + imag * cos)
                    for side in range(2):
                        at = side * width + c
                        rhs = jnp.concatenate(
                            [
                                stack_refs[n][r * w_count + q, :, at : at + size]
                                for r in range(ROUNDS)
                            ],
                            axis=0,
                        )
                        term = dot(jnp.concatenate(turned[side], axis=0), rhs)
                        total = term if total is None else total + term
        at = pl.ds(pl.multiple_of(step * rows, LAG_STEP * rows), LAG_STEP * rows)
        if not first:
            total = total + total_ref[at, :]
        if not last:
            out_ref[at, :] = total
            return carry
        for t in range(LAG_STEP):
            lanes = pl.ds(pl.multiple_of((step + t) * block, block), block)
            for side in range(ROUNDS):
                part = total[t * rows : (t + 1) * rows, side * block : (side + 1) * block]
                stage_ref[rounds[side], :, lanes] = (part * scales[side]).astype(jnp.bfloat16)
        copy(index).start()
        return carry

    def copy(index):
        size = LAG_STEP * block
        lanes = pl.ds(pl.multiple_of(index * size, size), size)
        return pltpu.make_async_copy(
            stage_ref.at[:, :, lanes], out_ref.at[:, :, lanes], copy_sems.at[index]
        )

    lax.fori_loop(0, LAGS // LAG_STEP, one_step, 0)
    if last:
        for index in range(LAGS // LAG_STEP):
            copy(index).wait()


def correlate(state, masks, matching, shift, pieces, last):
    first = state is None
    own, plan = [], []
    for rows, first_bin, stack in pieces:
        if not any(rows is seen for seen in own):
            own.append(rows)
        at = next(n for n, seen in enumerate(own) if seen is rows)
        plan.append((at, first_bin, stack.shape[2] // 2))
    w_count, rows, two_bins = own[0].shape
    block = pieces[0][2].shape[1]
    cos, sin = tables(two_bins // 2)
    arrays = [jnp.asarray(cos), jnp.asarray(sin)]
    specs = [VMEM] * 2
    if first:
        arrays += [masks, matching]
        specs += [VMEM, SMEM]
    else:
        arrays.append(state[0])
        specs.append(VMEM)
    if last:
        arrays += [state[1], matching]
        specs += [VMEM, SMEM]
    others = own + [stack for *_, stack in pieces]
    shape = jax.ShapeDtypeStruct
    running = shape((LAGS * rows, ROUNDS * block), jnp.float32)
    scratch = []
    if last:
        final = shape((ROUNDS, rows, LAGS * block), jnp.bfloat16)
        outs, out_specs = [final], [pl.BlockSpec(memory_space=pl.ANY)]
        scratch = [
            pltpu.VMEM(final.shape, final.dtype),
            pltpu.SemaphoreType.DMA((LAGS // LAG_STEP,)),
        ]
    elif first:
        outs, out_specs = [running, shape((ROUNDS, rows, block), jnp.float32)], [VMEM] * 2
        scratch = [pltpu.VMEM((block, block), jnp.float32)]
    else:
        outs, out_specs = [running], [VMEM]
    depth = 2 * sum(w_count * width for _, _, width in plan)
    result = pl.pallas_call(
        functools.partial(correlate_kernel, plan, shift, first, last),
        out_shape=outs,
        in_specs=specs + [VMEM] * len(others),
        out_specs=out_specs,
        scratch_shapes=scratch,
        compiler_params=PARAMS,
        cost_estimate=pl.CostEstimate(
            flops=2 * LAGS * rows * depth * ROUNDS * block,
            bytes_accessed=depth * (ROUNDS * block + rows) * 2,
            transcendentals=0,
        ),
    )(*arrays, *others)
    if last:
        return result[0]
    return (result[0], result[1] if first else state[1])


def combine(masks, matching, shift, own, sides):
    width = sides[0][0].shape[2] // 2
    low = descending_bits(lax.axis_size("win"))[-1]
    steps = [(d, n) for d in sorted(own) if not d & low for n in range(len(sides))]
    state, held = None, {}

    def stack(d, n, state):
        if (d, n) not in held:
            if d == 0:
                pair = sides[n]
                if state is not None:
                    pair, state = after(pair, state)
                held[d, n] = jnp.concatenate(pair, axis=0)
            else:
                bit = d & -d
                before, state = stack(d ^ bit, n, state)
                held[d, n] = flip(before, "win", bit)
        return held[d, n], state

    for number, (d, n) in enumerate(steps):
        here, state = stack(d, n, state)
        across = flip(here, "win", low)
        ahead = number + 1
        if 0 < number and ahead < len(steps) and steps[ahead][0] != 0:
            coming, state = stack(*steps[ahead], state)
            (held[steps[ahead]], across), state = after((coming, across), state)
        pieces = [(own[d], n * width, here), (own[d | low], n * width, across)]
        state = correlate(state, masks, matching, shift, pieces, ahead == len(steps))
    return state


def shards(spectra, masks, matching):
    blocks = lax.axis_size("chan")
    whole, parts, pair = prepare(spectra, masks, matching)

    if blocks > SWITCH_BLOCKS:
        sides = []
        for part in parts:
            left = right = part
            for bit in range(blocks.bit_length() - 1):
                taken = (matching[0, 0] >> bit) & 1 == 1
                moved = flip(jnp.where(taken, left, right), "chan", 1 << bit)
                left, right = jnp.where(taken, moved, left), jnp.where(taken, right, moved)
            sides.append([left, right])
        return combine(masks, matching, None, own_rows(whole, None)[0], sides)

    def branch(shift):
        def run(whole, parts):
            own, later = own_rows(whole, parts[1:])
            shifts = (shift, shift ^ (blocks - 1))
            sides = [[flip(part, "chan", s) for s in shifts] for part in (parts[0], *later)]
            return combine(masks, matching, shift, own, sides)

        return run

    return lax.switch(pair, [branch(s) for s in range(blocks // 2)], whole, parts)


def solution(mesh):
    in_specs = (P("win", "chan", None), P(), P())
    out_specs = P(None, ("chan", "win"), None)
    return jax.shard_map(shards, mesh=mesh, in_specs=in_specs, out_specs=out_specs, check_vma=False)
```

```python
import functools
import math

import jax
import jax.numpy as jnp
import numpy as np
from jax import lax
from jax.experimental import pallas as pl
from jax.experimental.pallas import tpu as pltpu
from jax.sharding import PartitionSpec as P

LAGS = 64
ROUNDS = 2
LAG_STEP = 16
LAST_LAG_STEP = 32
BIN_STEP = 256
PARTS = 2
SWITCH_BLOCKS = 8

VMEM = pl.BlockSpec(memory_space=pltpu.VMEM)
SMEM = pl.BlockSpec(memory_space=pltpu.SMEM)
PARAMS = pltpu.CompilerParams(vmem_limit_bytes=24 * 2**20)


def flip(value, axis, bits):
    if bits == 0:
        return value
    return lax.ppermute(value, axis, [(i, i ^ bits) for i in range(lax.axis_size(axis))])


def tables(bin_count):
    phase = np.arange(LAGS)[:, None] * np.arange(bin_count)[None, :] % (2 * bin_count)
    angle = phase.astype(np.float64) * (math.pi / bin_count)
    return np.cos(angle).astype(np.float32), np.sin(angle).astype(np.float32)


def descending_bits(size):
    return [1 << k for k in reversed(range(size.bit_length() - 1))]


def after(values, state):
    return lax.optimization_barrier((values, state))


def own_rows(values, later):
    held = {0: values}
    count = values.shape[0]
    for bit in descending_bits(lax.axis_size("win")):
        upper = (lax.axis_index("win") & bit) != 0
        half = held[0].shape[1] // 2
        kept, sent = {}, {}
        for d, rows in held.items():
            low, high = rows[:, :half], rows[:, half:]
            kept[d] = jnp.where(upper, high, low)
            sent[d] = jnp.where(upper, low, high)
        keys = list(held)
        moved = flip(jnp.concatenate([sent[d] for d in keys], axis=0), "win", bit)
        if len(keys) == 1 and later is not None:
            moved, later = after(moved, later)
        for n, d in enumerate(keys):
            kept[d | bit] = moved[n * count : (n + 1) * count]
        held = kept
    return held, later


def prepare_kernel(spectra_ref, masks_ref, matching_ref, whole_ref, *refs):
    part_refs, pair_ref = refs[:-1], refs[-1]
    w_count, block, two_bins = spectra_ref.shape
    bins = two_bins // 2
    first = matching_ref[0, 0]
    pair_ref[0] = jnp.minimum(first, first ^ (lax.axis_size("chan") - 1))
    at = pl.ds(pl.multiple_of(lax.axis_index("chan") * block, block), block)
    every = masks_ref[:, at].astype(jnp.float32)
    for q in range(w_count):
        window = lax.axis_index("win") * w_count + q
        chosen = lax.broadcasted_iota(jnp.int32, every.shape, 0) == window
        flags = lax.dot_general(
            every,
            chosen.astype(jnp.float32),
            (((0,), (0,)), ((), ())),
            preferred_element_type=jnp.float32,
        )
        chunk = 32
        for c in range(0, block, chunk):
            values = spectra_ref[q, c : c + chunk, :].astype(jnp.float32)
            mean_square = jnp.mean(values * values, axis=-1, keepdims=True)
            factor = flags[c : c + chunk, :1] * lax.rsqrt(mean_square + 1e-06)
            white = (values * factor).astype(jnp.bfloat16)
            whole_ref[q, c : c + chunk, :] = white
            for n, part_ref in enumerate(part_refs):
                width = part_ref.shape[2] // 2
                for side in range(2):
                    part_ref[q, c : c + chunk, side * width : (side + 1) * width] = white[
                        :, side * bins + n * width : side * bins + (n + 1) * width
                    ]


def prepare(spectra, masks, matching):
    w_count, block, two_bins = spectra.shape
    shape = jax.ShapeDtypeStruct
    part = shape((w_count, block, two_bins // PARTS), jnp.bfloat16)
    outs = pl.pallas_call(
        prepare_kernel,
        out_shape=[shape(spectra.shape, jnp.bfloat16)] + [part] * PARTS + [shape((1,), jnp.int32)],
        in_specs=[VMEM, VMEM, SMEM],
        out_specs=[VMEM] * (1 + PARTS) + [SMEM],
        compiler_params=PARAMS,
    )(spectra, masks, matching)
    return outs[0], outs[1:-1], outs[-1][0]


def correlate_kernel(plan, shift, first, last, *refs):
    refs = list(refs)
    lag_step = LAST_LAG_STEP if last else LAG_STEP
    take = lambda count: [refs.pop(0) for _ in range(count)]
    cos_ref, sin_ref = take(2)
    if first:
        masks_ref, matching_ref = take(2)
    else:
        (total_ref,) = take(1)
    if last:
        scale_ref, matching_ref = take(2)
    own_refs = take(1 + max(piece[0] for piece in plan))
    stack_refs = take(len(plan))
    w_count, rows, _ = own_refs[0].shape
    block = stack_refs[0].shape[1]
    bins = own_refs[0].shape[2] // 2

    def dot(lhs, rhs):
        return lax.dot_general(
            lhs, rhs, (((1,), (1,)), ((), ())), preferred_element_type=jnp.float32
        )

    if first:
        new_scale_ref, counts_ref = refs[1], refs[2]
        block_id, slot = lax.axis_index("chan"), lax.axis_index("win")
        own_at = pl.ds(pl.multiple_of(block_id * block, block), block)
        own_flags = masks_ref[:, own_at].astype(jnp.float32)
        for r in range(ROUNDS):
            partner = block_id ^ matching_ref[r, 0]
            at = pl.ds(pl.multiple_of(partner * block, block), block)
            counts = lax.dot_general(
                own_flags,
                masks_ref[:, at].astype(jnp.float32),
                (((0,), (0,)), ((), ())),
                preferred_element_type=jnp.float32,
            )
            counts_ref[...] = lax.rsqrt(bins * jnp.maximum(counts, 1.0))
            new_scale_ref[r] = counts_ref[pl.ds(pl.multiple_of(slot * rows, rows), rows), :]
    out_ref = refs[0]
    if last:
        stage_ref, copy_sems = refs[1], refs[2]
        swapped = 0 if shift is None else jnp.where(matching_ref[0, 0] == shift, 0, 1)
        rounds = [swapped, 1 - swapped]
        scales = [scale_ref[r] for r in rounds]

    def one_step(index, carry):
        step = pl.multiple_of(index * lag_step, lag_step)
        total = None
        for n, (own_at, first_bin, width) in enumerate(plan):
            for q in range(w_count):
                for c in range(0, width, BIN_STEP):
                    size = min(BIN_STEP, width - c)
                    b = first_bin + c
                    real = own_refs[own_at][q, :, b : b + size]
                    imag = own_refs[own_at][q, :, bins + b : bins + b + size]
                    cosine = cos_ref[pl.ds(step, lag_step), b : b + size].astype(jnp.bfloat16)
                    sine = sin_ref[pl.ds(step, lag_step), b : b + size].astype(jnp.bfloat16)
                    turned = [[], []]
                    for t in range(lag_step):
                        cos, sin = cosine[t : t + 1], sine[t : t + 1]
                        turned[0].append(real * cos - imag * sin)
                        turned[1].append(real * sin + imag * cos)
                    for side in range(2):
                        at = side * width + c
                        rhs = jnp.concatenate(
                            [
                                stack_refs[n][r * w_count + q, :, at : at + size]
                                for r in range(ROUNDS)
                            ],
                            axis=0,
                        )
                        term = dot(jnp.concatenate(turned[side], axis=0), rhs)
                        total = term if total is None else total + term
        at = pl.ds(pl.multiple_of(step * rows, lag_step * rows), lag_step * rows)
        if not first:
            total = total + total_ref[at, :]
        if not last:
            out_ref[at, :] = total
            return carry
        for t in range(lag_step):
            lanes = pl.ds(pl.multiple_of((step + t) * block, block), block)
            for side in range(ROUNDS):
                part = total[t * rows : (t + 1) * rows, side * block : (side + 1) * block]
                stage_ref[rounds[side], :, lanes] = (part * scales[side]).astype(jnp.bfloat16)
        copy(index).start()
        return carry

    def copy(index):
        size = lag_step * block
        lanes = pl.ds(pl.multiple_of(index * size, size), size)
        return pltpu.make_async_copy(
            stage_ref.at[:, :, lanes], out_ref.at[:, :, lanes], copy_sems.at[index]
        )

    lax.fori_loop(0, LAGS // lag_step, one_step, 0)
    if last:
        for index in range(LAGS // lag_step):
            copy(index).wait()


def correlate(state, masks, matching, shift, pieces, last):
    first = state is None
    own, plan = [], []
    for rows, first_bin, stack in pieces:
        if not any(rows is seen for seen in own):
            own.append(rows)
        at = next(n for n, seen in enumerate(own) if seen is rows)
        plan.append((at, first_bin, stack.shape[2] // 2))
    w_count, rows, two_bins = own[0].shape
    block = pieces[0][2].shape[1]
    cos, sin = tables(two_bins // 2)
    arrays = [jnp.asarray(cos), jnp.asarray(sin)]
    specs = [VMEM] * 2
    if first:
        arrays += [masks, matching]
        specs += [VMEM, SMEM]
    else:
        arrays.append(state[0])
        specs.append(VMEM)
    if last:
        arrays += [state[1], matching]
        specs += [VMEM, SMEM]
    others = own + [stack for *_, stack in pieces]
    shape = jax.ShapeDtypeStruct
    running = shape((LAGS * rows, ROUNDS * block), jnp.float32)
    scratch = []
    if last:
        final = shape((ROUNDS, rows, LAGS * block), jnp.bfloat16)
        outs, out_specs = [final], [pl.BlockSpec(memory_space=pl.ANY)]
        scratch = [
            pltpu.VMEM(final.shape, final.dtype),
            pltpu.SemaphoreType.DMA((LAGS // LAST_LAG_STEP,)),
        ]
    elif first:
        outs, out_specs = [running, shape((ROUNDS, rows, block), jnp.float32)], [VMEM] * 2
        scratch = [pltpu.VMEM((block, block), jnp.float32)]
    else:
        outs, out_specs = [running], [VMEM]
    depth = 2 * sum(w_count * width for _, _, width in plan)
    result = pl.pallas_call(
        functools.partial(correlate_kernel, plan, shift, first, last),
        out_shape=outs,
        in_specs=specs + [VMEM] * len(others),
        out_specs=out_specs,
        scratch_shapes=scratch,
        compiler_params=PARAMS,
        cost_estimate=pl.CostEstimate(
            flops=2 * LAGS * rows * depth * ROUNDS * block,
            bytes_accessed=depth * (ROUNDS * block + rows) * 2,
            transcendentals=0,
        ),
    )(*arrays, *others)
    if last:
        return result[0]
    return (result[0], result[1] if first else state[1])


def combine(masks, matching, shift, own, sides):
    width = sides[0][0].shape[2] // 2
    low = descending_bits(lax.axis_size("win"))[-1]
    steps = [(d, n) for d in sorted(own) if not d & low for n in range(len(sides))]
    state, held = None, {}

    def stack(d, n, state):
        if (d, n) not in held:
            if d == 0:
                pair = sides[n]
                if state is not None:
                    pair, state = after(pair, state)
                held[d, n] = jnp.concatenate(pair, axis=0)
            else:
                bit = d & -d
                before, state = stack(d ^ bit, n, state)
                held[d, n] = flip(before, "win", bit)
        return held[d, n], state

    early = set()
    for number, (d, n) in enumerate(steps):
        here, state = stack(d, n, state)
        across = flip(here, "win", low)
        pieces = [] if (d, n) in early else [(own[d], n * width, here)]
        ahead = number + 1
        if 0 < number and ahead < len(steps) and steps[ahead][0] != 0:
            coming, state = stack(*steps[ahead], state)
            (coming, across), state = after((coming, across), state)
            held[steps[ahead]] = coming
            early.add(steps[ahead])
            pieces.append((own[steps[ahead][0]], steps[ahead][1] * width, coming))
        pieces.append((own[d | low], n * width, across))
        state = correlate(state, masks, matching, shift, pieces, ahead == len(steps))
    return state


def shards(spectra, masks, matching):
    blocks = lax.axis_size("chan")
    whole, parts, pair = prepare(spectra, masks, matching)

    if blocks > SWITCH_BLOCKS:
        sides = []
        for part in parts:
            left = right = part
            for bit in range(blocks.bit_length() - 1):
                taken = (matching[0, 0] >> bit) & 1 == 1
                moved = flip(jnp.where(taken, left, right), "chan", 1 << bit)
                left, right = jnp.where(taken, moved, left), jnp.where(taken, right, moved)
            sides.append([left, right])
        return combine(masks, matching, None, own_rows(whole, None)[0], sides)

    def branch(shift):
        def run(whole, parts):
            own, later = own_rows(whole, parts[1:])
            shifts = (shift, shift ^ (blocks - 1))
            sides = [[flip(part, "chan", s) for s in shifts] for part in (parts[0], *later)]
            return combine(masks, matching, shift, own, sides)

        return run

    return lax.switch(pair, [branch(s) for s in range(blocks // 2)], whole, parts)


def solution(mesh):
    in_specs = (P("win", "chan", None), P(), P())
    out_specs = P(None, ("chan", "win"), None)
    return jax.shard_map(shards, mesh=mesh, in_specs=in_specs, out_specs=out_specs, check_vma=False)
```

```python
import functools
import math

import jax
import jax.numpy as jnp
import numpy as np
from jax import lax
from jax.experimental import pallas as pl
from jax.experimental.pallas import tpu as pltpu
from jax.sharding import PartitionSpec as P

LAGS = 64
ROUNDS = 2
LAG_STEP = 16
LONG_LAG_STEP = 32
BIN_STEP = 256
PARTS = 2
SWITCH_BLOCKS = 8

VMEM = pl.BlockSpec(memory_space=pltpu.VMEM)
SMEM = pl.BlockSpec(memory_space=pltpu.SMEM)
PARAMS = pltpu.CompilerParams(vmem_limit_bytes=24 * 2**20)


def flip(value, axis, bits):
    if bits == 0:
        return value
    return lax.ppermute(value, axis, [(i, i ^ bits) for i in range(lax.axis_size(axis))])


def tables(bin_count):
    phase = np.arange(LAGS)[:, None] * np.arange(bin_count)[None, :] % (2 * bin_count)
    angle = phase.astype(np.float64) * (math.pi / bin_count)
    return np.cos(angle).astype(np.float32), np.sin(angle).astype(np.float32)


def descending_bits(size):
    return [1 << k for k in reversed(range(size.bit_length() - 1))]


def after(values, state):
    return lax.optimization_barrier((values, state))


def own_rows(values, later):
    held = {0: values}
    count = values.shape[0]
    for bit in descending_bits(lax.axis_size("win")):
        upper = (lax.axis_index("win") & bit) != 0
        half = held[0].shape[1] // 2
        kept, sent = {}, {}
        for d, rows in held.items():
            low, high = rows[:, :half], rows[:, half:]
            kept[d] = jnp.where(upper, high, low)
            sent[d] = jnp.where(upper, low, high)
        keys = list(held)
        moved = flip(jnp.concatenate([sent[d] for d in keys], axis=0), "win", bit)
        if len(keys) == 1 and later is not None:
            moved, later = after(moved, later)
        for n, d in enumerate(keys):
            kept[d | bit] = moved[n * count : (n + 1) * count]
        held = kept
    return held, later


def prepare_kernel(spectra_ref, masks_ref, matching_ref, whole_ref, *refs):
    part_refs, pair_ref = refs[:-1], refs[-1]
    w_count, block, two_bins = spectra_ref.shape
    bins = two_bins // 2
    first = matching_ref[0, 0]
    pair_ref[0] = jnp.minimum(first, first ^ (lax.axis_size("chan") - 1))
    at = pl.ds(pl.multiple_of(lax.axis_index("chan") * block, block), block)
    every = masks_ref[:, at].astype(jnp.float32)
    for q in range(w_count):
        window = lax.axis_index("win") * w_count + q
        chosen = lax.broadcasted_iota(jnp.int32, every.shape, 0) == window
        flags = lax.dot_general(
            every,
            chosen.astype(jnp.float32),
            (((0,), (0,)), ((), ())),
            preferred_element_type=jnp.float32,
        )
        chunk = 32
        for c in range(0, block, chunk):
            values = spectra_ref[q, c : c + chunk, :].astype(jnp.float32)
            mean_square = jnp.mean(values * values, axis=-1, keepdims=True)
            factor = flags[c : c + chunk, :1] * lax.rsqrt(mean_square + 1e-06)
            white = (values * factor).astype(jnp.bfloat16)
            whole_ref[q, c : c + chunk, :] = white
            for n, part_ref in enumerate(part_refs):
                width = part_ref.shape[2] // 2
                for side in range(2):
                    part_ref[q, c : c + chunk, side * width : (side + 1) * width] = white[
                        :, side * bins + n * width : side * bins + (n + 1) * width
                    ]


def prepare(spectra, masks, matching):
    w_count, block, two_bins = spectra.shape
    shape = jax.ShapeDtypeStruct
    part = shape((w_count, block, two_bins // PARTS), jnp.bfloat16)
    outs = pl.pallas_call(
        prepare_kernel,
        out_shape=[shape(spectra.shape, jnp.bfloat16)] + [part] * PARTS + [shape((1,), jnp.int32)],
        in_specs=[VMEM, VMEM, SMEM],
        out_specs=[VMEM] * (1 + PARTS) + [SMEM],
        compiler_params=PARAMS,
    )(spectra, masks, matching)
    return outs[0], outs[1:-1], outs[-1][0]


def correlate_kernel(plan, shift, first, scaling, last, *refs):
    refs = list(refs)
    lag_step = LONG_LAG_STEP if len(plan) < 3 else LAG_STEP
    take = lambda count: [refs.pop(0) for _ in range(count)]
    cos_ref, sin_ref = take(2)
    if not first:
        (total_ref,) = take(1)
    if scaling:
        masks_ref, matching_ref = take(2)
    if last:
        scale_ref, matching_ref = take(2)
    own_refs = take(1 + max(piece[0] for piece in plan))
    stack_refs = take(len(plan))
    w_count, rows, _ = own_refs[0].shape
    block = stack_refs[0].shape[1]
    bins = own_refs[0].shape[2] // 2

    def dot(lhs, rhs):
        return lax.dot_general(
            lhs, rhs, (((1,), (1,)), ((), ())), preferred_element_type=jnp.float32
        )

    if scaling:
        new_scale_ref, counts_ref = refs[1], refs[2]
        block_id, slot = lax.axis_index("chan"), lax.axis_index("win")
        own_at = pl.ds(pl.multiple_of(block_id * block, block), block)
        own_flags = masks_ref[:, own_at].astype(jnp.float32)
        for r in range(ROUNDS):
            partner = block_id ^ matching_ref[r, 0]
            at = pl.ds(pl.multiple_of(partner * block, block), block)
            counts = lax.dot_general(
                own_flags,
                masks_ref[:, at].astype(jnp.float32),
                (((0,), (0,)), ((), ())),
                preferred_element_type=jnp.float32,
            )
            counts_ref[...] = lax.rsqrt(bins * jnp.maximum(counts, 1.0))
            new_scale_ref[r] = counts_ref[pl.ds(pl.multiple_of(slot * rows, rows), rows), :]
    out_ref = refs[0]
    if last:
        stage_ref, copy_sems = refs[1], refs[2]
        swapped = 0 if shift is None else jnp.where(matching_ref[0, 0] == shift, 0, 1)
        rounds = [swapped, 1 - swapped]
        scales = [scale_ref[r] for r in rounds]

    def one_step(index, carry):
        step = pl.multiple_of(index * lag_step, lag_step)
        total = None
        for n, (own_at, first_bin, width) in enumerate(plan):
            for q in range(w_count):
                for c in range(0, width, BIN_STEP):
                    size = min(BIN_STEP, width - c)
                    b = first_bin + c
                    real = own_refs[own_at][q, :, b : b + size]
                    imag = own_refs[own_at][q, :, bins + b : bins + b + size]
                    cosine = cos_ref[pl.ds(step, lag_step), b : b + size].astype(jnp.bfloat16)
                    sine = sin_ref[pl.ds(step, lag_step), b : b + size].astype(jnp.bfloat16)
                    turned = [[], []]
                    for t in range(lag_step):
                        cos, sin = cosine[t : t + 1], sine[t : t + 1]
                        turned[0].append(real * cos - imag * sin)
                        turned[1].append(real * sin + imag * cos)
                    for side in range(2):
                        at = side * width + c
                        rhs = jnp.concatenate(
                            [
                                stack_refs[n][r * w_count + q, :, at : at + size]
                                for r in range(ROUNDS)
                            ],
                            axis=0,
                        )
                        term = dot(jnp.concatenate(turned[side], axis=0), rhs)
                        total = term if total is None else total + term
        at = pl.ds(pl.multiple_of(step * rows, lag_step * rows), lag_step * rows)
        if not first:
            total = total + total_ref[at, :]
        if not last:
            out_ref[at, :] = total
            return carry
        for t in range(lag_step):
            lanes = pl.ds(pl.multiple_of((step + t) * block, block), block)
            for side in range(ROUNDS):
                part = total[t * rows : (t + 1) * rows, side * block : (side + 1) * block]
                stage_ref[rounds[side], :, lanes] = (part * scales[side]).astype(jnp.bfloat16)
        copy(index).start()
        return carry

    def copy(index):
        size = lag_step * block
        lanes = pl.ds(pl.multiple_of(index * size, size), size)
        return pltpu.make_async_copy(
            stage_ref.at[:, :, lanes], out_ref.at[:, :, lanes], copy_sems.at[index]
        )

    lax.fori_loop(0, LAGS // lag_step, one_step, 0)
    if last:
        for index in range(LAGS // lag_step):
            copy(index).wait()


def correlate(state, masks, matching, shift, pieces, scaling, last):
    first = state is None
    own, plan = [], []
    for rows, first_bin, stack in pieces:
        if not any(rows is seen for seen in own):
            own.append(rows)
        at = next(n for n, seen in enumerate(own) if seen is rows)
        plan.append((at, first_bin, stack.shape[2] // 2))
    w_count, rows, two_bins = own[0].shape
    block = pieces[0][2].shape[1]
    cos, sin = tables(two_bins // 2)
    arrays = [jnp.asarray(cos), jnp.asarray(sin)]
    specs = [VMEM] * 2
    if not first:
        arrays.append(state[0])
        specs.append(VMEM)
    if scaling:
        arrays += [masks, matching]
        specs += [VMEM, SMEM]
    if last:
        arrays += [state[1], matching]
        specs += [VMEM, SMEM]
    others = own + [stack for *_, stack in pieces]
    shape = jax.ShapeDtypeStruct
    running = shape((LAGS * rows, ROUNDS * block), jnp.float32)
    scratch = []
    if last:
        final = shape((ROUNDS, rows, LAGS * block), jnp.bfloat16)
        outs, out_specs = [final], [pl.BlockSpec(memory_space=pl.ANY)]
        scratch = [
            pltpu.VMEM(final.shape, final.dtype),
            pltpu.SemaphoreType.DMA((LAGS // LONG_LAG_STEP,)),
        ]
    elif scaling:
        outs, out_specs = [running, shape((ROUNDS, rows, block), jnp.float32)], [VMEM] * 2
        scratch = [pltpu.VMEM((block, block), jnp.float32)]
    else:
        outs, out_specs = [running], [VMEM]
    depth = 2 * sum(w_count * width for _, _, width in plan)
    result = pl.pallas_call(
        functools.partial(correlate_kernel, plan, shift, first, scaling, last),
        out_shape=outs,
        in_specs=specs + [VMEM] * len(others),
        out_specs=out_specs,
        scratch_shapes=scratch,
        compiler_params=PARAMS,
        cost_estimate=pl.CostEstimate(
            flops=2 * LAGS * rows * depth * ROUNDS * block,
            bytes_accessed=depth * (ROUNDS * block + rows) * 2,
            transcendentals=0,
        ),
    )(*arrays, *others)
    if last:
        return result[0]
    return [result[0], *(result[1:] if scaling else [] if first else state[1:])]


def combine(masks, matching, shift, own, sides):
    width = sides[0][0].shape[2] // 2
    low = descending_bits(lax.axis_size("win"))[-1]
    steps = [(d, n) for d in sorted(own) if not d & low for n in range(len(sides))]
    state, held = None, {}

    def stack(d, n, state):
        if (d, n) not in held:
            if d == 0:
                pair = sides[n]
                if state is not None:
                    pair, state = after(pair, state)
                held[d, n] = jnp.concatenate(pair, axis=0)
            else:
                bit = d & -d
                before, state = stack(d ^ bit, n, state)
                held[d, n] = flip(before, "win", bit)
        return held[d, n], state

    early = set()
    for number, (d, n) in enumerate(steps):
        here, state = stack(d, n, state)
        across = flip(here, "win", low)
        pieces = [] if (d, n) in early else [(own[d], n * width, here)]
        ahead = number + 1
        if 0 < number and ahead < len(steps) and steps[ahead][0] != 0:
            coming, state = stack(*steps[ahead], state)
            (coming, across), state = after((coming, across), state)
            held[steps[ahead]] = coming
            early.add(steps[ahead])
            pieces.append((own[steps[ahead][0]], steps[ahead][1] * width, coming))
        pieces.append((own[d | low], n * width, across))
        state = correlate(state, masks, matching, shift, pieces, number == 1, ahead == len(steps))
    return state


def shards(spectra, masks, matching):
    blocks = lax.axis_size("chan")
    whole, parts, pair = prepare(spectra, masks, matching)

    if blocks > SWITCH_BLOCKS:
        sides = []
        for part in parts:
            left = right = part
            for bit in range(blocks.bit_length() - 1):
                taken = (matching[0, 0] >> bit) & 1 == 1
                moved = flip(jnp.where(taken, left, right), "chan", 1 << bit)
                left, right = jnp.where(taken, moved, left), jnp.where(taken, right, moved)
            sides.append([left, right])
        return combine(masks, matching, None, own_rows(whole, None)[0], sides)

    def branch(shift):
        def run(whole, parts):
            own, later = own_rows(whole, parts[1:])
            shifts = (shift, shift ^ (blocks - 1))
            sides = [[flip(part, "chan", s) for s in shifts] for part in (parts[0], *later)]
            return combine(masks, matching, shift, own, sides)

        return run

    return lax.switch(pair, [branch(s) for s in range(blocks // 2)], whole, parts)


def solution(mesh):
    in_specs = (P("win", "chan", None), P(), P())
    out_specs = P(None, ("chan", "win"), None)
    return jax.shard_map(shards, mesh=mesh, in_specs=in_specs, out_specs=out_specs, check_vma=False)
```

```python
import functools
import math

import jax
import jax.numpy as jnp
import numpy as np
from jax import lax
from jax.experimental import pallas as pl
from jax.experimental.pallas import tpu as pltpu
from jax.sharding import PartitionSpec as P

LAGS = 64
ROUNDS = 2
LAG_STEP = 16
LONG_LAG_STEP = 32
BIN_STEP = 256
PARTS = 2
SWITCH_BLOCKS = 8

VMEM = pl.BlockSpec(memory_space=pltpu.VMEM)
SMEM = pl.BlockSpec(memory_space=pltpu.SMEM)
PARAMS = pltpu.CompilerParams(vmem_limit_bytes=24 * 2**20)


def flip(value, axis, bits):
    if bits == 0:
        return value
    return lax.ppermute(value, axis, [(i, i ^ bits) for i in range(lax.axis_size(axis))])


def tables(bin_count):
    phase = np.arange(LAGS)[:, None] * np.arange(bin_count)[None, :] % (2 * bin_count)
    angle = phase.astype(np.float64) * (math.pi / bin_count)
    return np.cos(angle).astype(np.float32), np.sin(angle).astype(np.float32)


def descending_bits(size):
    return [1 << k for k in reversed(range(size.bit_length() - 1))]


def after(values, state):
    return lax.optimization_barrier((values, state))


def own_rows(values, later):
    held = {0: values}
    count = values.shape[0]
    for bit in descending_bits(lax.axis_size("win")):
        upper = (lax.axis_index("win") & bit) != 0
        half = held[0].shape[1] // 2
        kept, sent = {}, {}
        for d, rows in held.items():
            low, high = rows[:, :half], rows[:, half:]
            kept[d] = jnp.where(upper, high, low)
            sent[d] = jnp.where(upper, low, high)
        keys = list(held)
        moved = flip(jnp.concatenate([sent[d] for d in keys], axis=0), "win", bit)
        if len(keys) == 1 and later is not None:
            moved, later = after(moved, later)
        for n, d in enumerate(keys):
            kept[d | bit] = moved[n * count : (n + 1) * count]
        held = kept
    return held, later


def prepare_kernel(spectra_ref, masks_ref, matching_ref, whole_ref, *refs):
    part_refs, pair_ref = refs[:-1], refs[-1]
    w_count, block, two_bins = spectra_ref.shape
    bins = two_bins // 2
    first = matching_ref[0, 0]
    pair_ref[0] = jnp.minimum(first, first ^ (lax.axis_size("chan") - 1))
    at = pl.ds(pl.multiple_of(lax.axis_index("chan") * block, block), block)
    every = masks_ref[:, at].astype(jnp.float32)
    for q in range(w_count):
        window = lax.axis_index("win") * w_count + q
        chosen = lax.broadcasted_iota(jnp.int32, every.shape, 0) == window
        flags = lax.dot_general(
            every,
            chosen.astype(jnp.float32),
            (((0,), (0,)), ((), ())),
            preferred_element_type=jnp.float32,
        )
        chunk = 32
        for c in range(0, block, chunk):
            values = spectra_ref[q, c : c + chunk, :].astype(jnp.float32)
            mean_square = jnp.mean(values * values, axis=-1, keepdims=True)
            factor = flags[c : c + chunk, :1] * lax.rsqrt(mean_square + 1e-06)
            white = (values * factor).astype(jnp.bfloat16)
            whole_ref[q, c : c + chunk, :] = white
            for n, part_ref in enumerate(part_refs):
                width = part_ref.shape[2] // 2
                for side in range(2):
                    part_ref[q, c : c + chunk, side * width : (side + 1) * width] = white[
                        :, side * bins + n * width : side * bins + (n + 1) * width
                    ]


def prepare(spectra, masks, matching):
    w_count, block, two_bins = spectra.shape
    shape = jax.ShapeDtypeStruct
    part = shape((w_count, block, two_bins // PARTS), jnp.bfloat16)
    outs = pl.pallas_call(
        prepare_kernel,
        out_shape=[shape(spectra.shape, jnp.bfloat16)] + [part] * PARTS + [shape((1,), jnp.int32)],
        in_specs=[VMEM, VMEM, SMEM],
        out_specs=[VMEM] * (1 + PARTS) + [SMEM],
        compiler_params=PARAMS,
    )(spectra, masks, matching)
    return outs[0], outs[1:-1], outs[-1][0]


def correlate_kernel(plan, shift, first, scaling, last, *refs):
    refs = list(refs)
    lag_step = LONG_LAG_STEP if len(plan) < 3 else LAG_STEP
    take = lambda count: [refs.pop(0) for _ in range(count)]
    cos_ref, sin_ref = take(2)
    if not first:
        (total_ref,) = take(1)
    if scaling:
        masks_ref, matching_ref = take(2)
    if last:
        scale_ref, matching_ref = take(2)
    own_refs = take(1 + max(piece[0] for piece in plan))
    stack_refs = take(len(plan))
    w_count, rows, _ = own_refs[0].shape
    block = stack_refs[0].shape[1]
    bins = own_refs[0].shape[2] // 2

    def dot(lhs, rhs):
        return lax.dot_general(
            lhs, rhs, (((1,), (1,)), ((), ())), preferred_element_type=jnp.float32
        )

    if scaling:
        new_scale_ref, counts_ref = refs[1], refs[2]
        block_id, slot = lax.axis_index("chan"), lax.axis_index("win")
        own_at = pl.ds(pl.multiple_of(block_id * block, block), block)
        own_flags = masks_ref[:, own_at].astype(jnp.float32)
        for r in range(ROUNDS):
            partner = block_id ^ matching_ref[r, 0]
            at = pl.ds(pl.multiple_of(partner * block, block), block)
            counts = lax.dot_general(
                own_flags,
                masks_ref[:, at].astype(jnp.float32),
                (((0,), (0,)), ((), ())),
                preferred_element_type=jnp.float32,
            )
            counts_ref[...] = lax.rsqrt(bins * jnp.maximum(counts, 1.0))
            new_scale_ref[r] = counts_ref[pl.ds(pl.multiple_of(slot * rows, rows), rows), :]
    out_ref = refs[0]
    if last:
        stage_ref, copy_sems = refs[1], refs[2]
        swapped = 0 if shift is None else jnp.where(matching_ref[0, 0] == shift, 0, 1)
        rounds = [swapped, 1 - swapped]
        scales = [scale_ref[r] for r in rounds]

    def one_step(index, carry):
        step = pl.multiple_of(index * lag_step, lag_step)
        total = None
        for n, (own_at, first_bin, width) in enumerate(plan):
            for q in range(w_count):
                for c in range(0, width, BIN_STEP):
                    size = min(BIN_STEP, width - c)
                    b = first_bin + c
                    real = own_refs[own_at][q, :, b : b + size]
                    imag = own_refs[own_at][q, :, bins + b : bins + b + size]
                    cosine = cos_ref[pl.ds(step, lag_step), b : b + size].astype(jnp.bfloat16)
                    sine = sin_ref[pl.ds(step, lag_step), b : b + size].astype(jnp.bfloat16)
                    turned = [[], []]
                    for t in range(lag_step):
                        cos, sin = cosine[t : t + 1], sine[t : t + 1]
                        turned[0].append(real * cos - imag * sin)
                        turned[1].append(real * sin + imag * cos)
                    for side in range(2):
                        at = side * width + c
                        rhs = jnp.concatenate(
                            [
                                stack_refs[n][r * w_count + q, :, at : at + size]
                                for r in range(ROUNDS)
                            ],
                            axis=0,
                        )
                        term = dot(jnp.concatenate(turned[side], axis=0), rhs)
                        total = term if total is None else total + term
        at = pl.ds(pl.multiple_of(step * rows, lag_step * rows), lag_step * rows)
        if not first:
            total = total + total_ref[at, :]
        if not last:
            out_ref[at, :] = total
            return carry
        for t in range(lag_step):
            lanes = pl.ds(pl.multiple_of((step + t) * block, block), block)
            for side in range(ROUNDS):
                part = total[t * rows : (t + 1) * rows, side * block : (side + 1) * block]
                stage_ref[rounds[side], :, lanes] = (part * scales[side]).astype(jnp.bfloat16)
        copy(index).start()
        return carry

    def copy(index):
        size = lag_step * block
        lanes = pl.ds(pl.multiple_of(index * size, size), size)
        return pltpu.make_async_copy(
            stage_ref.at[:, :, lanes], out_ref.at[:, :, lanes], copy_sems.at[index]
        )

    lax.fori_loop(0, LAGS // lag_step, one_step, 0)
    if last:
        for index in range(LAGS // lag_step):
            copy(index).wait()


def correlate(state, masks, matching, shift, pieces, scaling, last):
    first = state is None
    own, plan = [], []
    for rows, first_bin, stack in pieces:
        if not any(rows is seen for seen in own):
            own.append(rows)
        at = next(n for n, seen in enumerate(own) if seen is rows)
        plan.append((at, first_bin, stack.shape[2] // 2))
    w_count, rows, two_bins = own[0].shape
    block = pieces[0][2].shape[1]
    cos, sin = tables(two_bins // 2)
    arrays = [jnp.asarray(cos), jnp.asarray(sin)]
    specs = [VMEM] * 2
    if not first:
        arrays.append(state[0])
        specs.append(VMEM)
    if scaling:
        arrays += [masks, matching]
        specs += [VMEM, SMEM]
    if last:
        arrays += [state[1], matching]
        specs += [VMEM, SMEM]
    others = own + [stack for *_, stack in pieces]
    shape = jax.ShapeDtypeStruct
    running = shape((LAGS * rows, ROUNDS * block), jnp.float32)
    scratch = []
    if last:
        final = shape((ROUNDS, rows, LAGS * block), jnp.bfloat16)
        outs, out_specs = [final], [pl.BlockSpec(memory_space=pl.ANY)]
        scratch = [
            pltpu.VMEM(final.shape, final.dtype),
            pltpu.SemaphoreType.DMA((LAGS // LONG_LAG_STEP,)),
        ]
    elif scaling:
        outs, out_specs = [running, shape((ROUNDS, rows, block), jnp.float32)], [VMEM] * 2
        scratch = [pltpu.VMEM((block, block), jnp.float32)]
    else:
        outs, out_specs = [running], [VMEM]
    depth = 2 * sum(w_count * width for _, _, width in plan)
    result = pl.pallas_call(
        functools.partial(correlate_kernel, plan, shift, first, scaling, last),
        out_shape=outs,
        in_specs=specs + [VMEM] * len(others),
        out_specs=out_specs,
        scratch_shapes=scratch,
        compiler_params=PARAMS,
        cost_estimate=pl.CostEstimate(
            flops=2 * LAGS * rows * depth * ROUNDS * block,
            bytes_accessed=depth * (ROUNDS * block + rows) * 2,
            transcendentals=0,
        ),
    )(*arrays, *others)
    if last:
        return result[0]
    return [result[0], *(result[1:] if scaling else [] if first else state[1:])]


def combine(masks, matching, shift, own, sides):
    width = sides[0][0].shape[2] // 2
    low = descending_bits(lax.axis_size("win"))[-1]
    steps = [(d, n) for d in sorted(own) if not d & low for n in range(len(sides))]
    state, held = None, {}

    def stack(d, n, state):
        if (d, n) not in held:
            if d == 0:
                pair = sides[n]
                if state is not None:
                    pair, state = after(pair, state)
                held[d, n] = jnp.concatenate(pair, axis=0)
            else:
                bit = d & -d
                before, state = stack(d ^ bit, n, state)
                held[d, n] = flip(before, "win", bit)
        return held[d, n], state

    early, waiting = set(), []
    for number, (d, n) in enumerate(steps):
        here, state = stack(d, n, state)
        across = flip(here, "win", low)
        if number == 0:
            here, own = after(here, own)
        pieces = waiting + ([] if (d, n) in early else [(own[d], n * width, here)])
        ahead = number + 1
        if 0 < number and ahead < len(steps) and steps[ahead][0] != 0:
            coming, state = stack(*steps[ahead], state)
            (coming, across), state = after((coming, across), state)
            held[steps[ahead]] = coming
            early.add(steps[ahead])
            pieces.append((own[steps[ahead][0]], steps[ahead][1] * width, coming))
        waiting = [(own[d | low], n * width, across)]
        if number > 0 or ahead == len(steps):
            pieces, waiting = pieces + waiting, []
        state = correlate(state, masks, matching, shift, pieces, number == 1, ahead == len(steps))
    return state


def shards(spectra, masks, matching):
    blocks = lax.axis_size("chan")
    whole, parts, pair = prepare(spectra, masks, matching)

    if blocks > SWITCH_BLOCKS:
        sides = []
        for part in parts:
            left = right = part
            for bit in range(blocks.bit_length() - 1):
                taken = (matching[0, 0] >> bit) & 1 == 1
                moved = flip(jnp.where(taken, left, right), "chan", 1 << bit)
                left, right = jnp.where(taken, moved, left), jnp.where(taken, right, moved)
            sides.append([left, right])
        return combine(masks, matching, None, own_rows(whole, None)[0], sides)

    def branch(shift):
        def run(whole, parts):
            own, later = own_rows(whole, parts[1:])
            shifts = (shift, shift ^ (blocks - 1))
            sides = [[flip(part, "chan", s) for s in shifts] for part in (parts[0], *later)]
            return combine(masks, matching, shift, own, sides)

        return run

    return lax.switch(pair, [branch(s) for s in range(blocks // 2)], whole, parts)


def solution(mesh):
    in_specs = (P("win", "chan", None), P(), P())
    out_specs = P(None, ("chan", "win"), None)
    return jax.shard_map(shards, mesh=mesh, in_specs=in_specs, out_specs=out_specs, check_vma=False)
```
